1024 devices in a mesh: grp: 8 (over y), sub: 128 (over z, x, core).
Axes of the slice: x: 4, y: 8, z: 16, core: 2. Of those that a mesh axis runs over, the one named last changes fastest.
Arguments:
- rhs: float32 [8, 128, 8, 2048], P('grp', 'sub'), may hold values from -6 to 6
- diagonal: float32 [8, 128, 2048], P('grp', 'sub'), may hold values from 3 to 6
- blocks: float32 [8, 128, 32, 3, 64, 64], P('grp', 'sub'), may hold values from -0.4375 to 0.4375
- pattern: int32 [8, 128, 32, 3], P('grp', 'sub'), may hold values from 0 to 31
- margin: int32 [8, 128, 4, 4], P('grp', 'sub'), may hold values from 0 to 15
- basis: float32 [8, 128, 48, 2048], P('grp', 'sub'), may hold values from -0.25 to 0.25
- coarse_inverse: float32 [8, 6144, 6144], P('grp', 'sub'), as said below
Outputs:
- solution: float32 [8, 128, 8, 2048], P('grp', 'sub')
The draws below stay inside these ranges and needn't reach their ends.
Inputs may be any that keep to these rules, and one draw needn't show every extreme that they name: `coarse_inverse`: each group's matrix is symmetric.
All inputs are finite; a program needn't handle non-finite values.
Results may differ from the reference program's by a relative error of at most 0.0003.
Values sent between devices are 32-bit elements; how exact they have to be, the bound alone decides.
No kernel may reach another device: no remote copies, remote signals or barrier semaphores. Data moves between devices by JAX's collectives and lax.ppermute only.
A program may use at most 32 MiB of HBM per device.

```python
import jax
import jax.numpy as jnp
from jax import lax

ROWS = 2048
NRHS = 8
BLK = 64
KNZ = 3
GEN = 48
OVB = 4
ITERS = 3
NBLK = 32
COARSE = 6144
N_GRP = 8
N_SUB = 128


def draw_coarse_inverse(key, part):
    key = jax.random.fold_in(key, 7)
    first, second = jax.random.split(key)
    noise = jax.random.normal(first, (N_GRP, COARSE, COARSE), jnp.float32)
    noise = (noise + jnp.swapaxes(noise, 1, 2)) * (0.6 / COARSE ** 0.5)
    scales = jax.random.uniform(second, (N_GRP, COARSE), jnp.float32, 0.5, 1.5)
    return noise + jnp.eye(COARSE, dtype=jnp.float32)[None] * scales[:, None, :]


def with_ends(array, own_key, smallest, top_value):
    place = [jax.random.randint(jax.random.fold_in(own_key, axis), (), 0, length) for axis, length in enumerate(array.shape)]
    widest = array.shape.index(max(array.shape))
    next_to = place[:widest] + [(place[widest] + 1) % array.shape[widest]] + place[widest + 1:]
    return array.at[tuple(place)].set(smallest).at[tuple(next_to)].set(top_value)


def block_scale(rng, dims, cuts, smallest, top_value):
    factor_of = 1.0
    for axis_at, blocks in cuts:
        steps = jax.random.uniform(jax.random.fold_in(jax.random.fold_in(rng, 6), axis_at), (blocks,), jnp.float32, smallest / len(cuts), top_value / len(cuts))
        factor_of = factor_of * jnp.repeat(jnp.exp(steps), dims[axis_at] // blocks).reshape((-1,) + (1,) * (len(dims) - 1 - axis_at))
    return factor_of


def bell_draw(rng, extent, deviation, limit, pieces=(), kind=jnp.bfloat16):
    array = jax.random.normal(rng, extent, jnp.float32) * deviation
    if len(pieces) > 0:
        array = block_scale(rng, extent, pieces, -0.22, 0.18) * array
    return jnp.clip(array, min=-limit, max=limit).astype(kind)


def setup_inputs(seed: int = 0) -> dict:
    key_of = jax.random.split(jax.random.key(seed), 8)
    rhs = bell_draw(key_of[0], (N_GRP, N_SUB, NRHS, ROWS), 1.0, 6.0, ((0, 8), (1, 128)), jnp.float32)
    diagonal = jnp.clip(3.0 + 3.0 * jax.random.uniform(key_of[1], (N_GRP, N_SUB, ROWS), jnp.float32) ** block_scale(key_of[1], (N_GRP, N_SUB, ROWS), ((0, 8), (1, 128)), -0.2, 0.2), 3.0, 6.0)
    blocks = bell_draw(key_of[2], (N_GRP, N_SUB, NBLK, KNZ, BLK, BLK), (BLK * KNZ) ** -0.5, 0.4375, ((0, 8), (1, 128)), jnp.float32)
    pattern = with_ends(jax.random.randint(key_of[3], (N_GRP, N_SUB, NBLK, KNZ), 0, NBLK), jax.random.fold_in(key_of[3], 1), 0, NBLK - 1).astype(jnp.int32)
    margin = with_ends(jax.random.randint(key_of[4], (N_GRP, N_SUB, 4, OVB), 0, ROWS // 128), jax.random.fold_in(key_of[4], 1), 0, (ROWS // 128) - 1).astype(jnp.int32)
    basis = bell_draw(key_of[5], (N_GRP, N_SUB, GEN, ROWS), (ROWS // 4) ** -0.5, 0.25, ((0, 8), (1, 128)), jnp.float32)
    coarse_inverse = draw_coarse_inverse(jax.random.fold_in(key_of[7], 71), 0)
    return {"rhs": rhs, "diagonal": diagonal, "blocks": blocks, "pattern": pattern, "margin": margin, "basis": basis, "coarse_inverse": coarse_inverse}


def least_squares(columns, beta):
    ortho = []
    upper = []
    for k in range(len(columns)):
        vector = columns[k]
        coeffs = []
        for i in range(k):
            weight = lax.optimization_barrier(jnp.sum(ortho[i] * columns[k], axis=-1))
            coeffs.append(weight)
            vector = vector - weight[:, None] * ortho[i]
        length = jnp.sqrt(lax.optimization_barrier(jnp.sum(vector * vector, axis=-1)))
        coeffs.append(length)
        upper.append(coeffs)
        ortho.append(vector / length[:, None])
    target = [ortho[k][:, 0] * beta for k in range(len(columns))]
    result = [None] * len(columns)
    for k in reversed(range(len(columns))):
        value = target[k]
        for i in range(k + 1, len(columns)):
            value = value - upper[i][k] * result[i]
        result[k] = value / upper[k][k]
    return result

def local_part(field, blocks, pattern, diagonal):
    shaped = field.reshape(NRHS, NBLK, BLK)
    picked = shaped[:, pattern]
    local = jnp.einsum('bkoi,nbki->nbo', blocks, picked, precision=lax.Precision.HIGHEST)
    return diagonal[None, :] * field + local.reshape(NRHS, ROWS)

def take_rims(field, margin):
    tiles = field.reshape(NRHS, ROWS // 128, 128)
    return tiles[:, margin].reshape(NRHS, 4, OVB * 128)

def put_rims(received, margin):
    zeros = jnp.zeros((NRHS, ROWS // 128, 128), jnp.float32)
    added = zeros.at[:, margin.reshape(-1)].add(received.reshape(NRHS, 4 * OVB, 128))
    return added.reshape(NRHS, ROWS)

def operate(field, blocks, pattern, diagonal, margin):
    base = jax.vmap(jax.vmap(local_part))(field, blocks, pattern, diagonal)
    send = jax.vmap(jax.vmap(take_rims))(field, margin)
    zero_g = jnp.zeros_like(send[:1, :, :, 0])
    from_low = jnp.concatenate([zero_g, send[:-1, :, :, 1]], axis=0)
    from_high = jnp.concatenate([send[1:, :, :, 0], zero_g], axis=0)
    zero_s = jnp.zeros_like(send[:, :1, :, 0])
    sub_low = jnp.concatenate([zero_s, send[:, :-1, :, 3]], axis=1)
    sub_high = jnp.concatenate([send[:, 1:, :, 2], zero_s], axis=1)
    received = jnp.stack([from_low, from_high, sub_low, sub_high], axis=3)
    return base - jax.vmap(jax.vmap(put_rims))(received, margin)

def precondition(field, diagonal, basis, coarse_inverse):
    groups = field.shape[0]
    subs = field.shape[1]
    coarse = jnp.einsum('gsmr,gsnr->gnsm', basis, field, precision=lax.Precision.HIGHEST)
    coarse = coarse.reshape(groups, NRHS, subs * GEN)
    answer = jnp.einsum('gcd,gnd->gnc', coarse_inverse, coarse, precision=lax.Precision.HIGHEST)
    answer = answer.reshape(groups, NRHS, subs, GEN)
    back = jnp.einsum('gsmr,gnsm->gsnr', basis, answer, precision=lax.Precision.HIGHEST)
    return field / diagonal[:, :, None, :] + back

def total(values):
    return lax.optimization_barrier(jnp.sum(values, axis=(0, 1, 3)))

def reference(rhs, diagonal, blocks, pattern, margin, basis, coarse_inverse):

    def expand(scalar):
        return scalar[None, None, :, None]
    beta = jnp.sqrt(total(rhs * rhs))
    vectors = [rhs / expand(beta)]
    columns = []
    for step in range(ITERS):
        image = operate(precondition(vectors[step], diagonal, basis, coarse_inverse), blocks, pattern, diagonal, margin)
        dots = [total(vec * image) for vec in vectors]
        square = total(image * image)
        rest = image
        heights = jnp.zeros_like(square)
        for i in range(step + 1):
            rest = rest - expand(dots[i]) * vectors[i]
            heights = heights + dots[i] * dots[i]
        height = jnp.sqrt(jnp.maximum(square - heights, 0.001 * square))
        entries = dots + [height] + [jnp.zeros_like(height)] * (ITERS - step - 1)
        columns.append(jnp.stack(entries, axis=-1))
        vectors.append(rest / expand(height))
    coeffs = least_squares(columns, beta)
    combo = jnp.zeros_like(rhs)
    for i in range(ITERS):
        combo = combo + expand(coeffs[i]) * vectors[i]
    return precondition(combo, diagonal, basis, coarse_inverse)
```

```python
import jax
import jax.numpy as jnp
from jax import lax
from jax.sharding import Mesh, PartitionSpec as P

ITERS = 3
SUB = ("z", "x", "core")
HIGH = lax.Precision.HIGHEST


def gathered(value, axis):
    size = lax.axis_size(axis)
    return lax.all_to_all(jnp.broadcast_to(value[None], (size,) + value.shape), axis, 0, 0)


def gather_coarse(piece):
    count, width = piece.shape
    pair = lax.all_gather(piece, "core", axis=1, tiled=True)
    whole = gathered(gathered(pair, "z"), "x")
    return jnp.transpose(whole, (2, 1, 0, 3)).reshape(count, -1)


def total(values):
    values = jnp.sum(gathered(values, ("x", "core")), axis=0)
    values = jnp.sum(gathered(values, "z"), axis=0)
    return jnp.sum(gathered(values, "grp"), axis=0)


def least_squares(columns, beta):
    ortho = []
    upper = []
    for k in range(len(columns)):
        vector = columns[k]
        coeffs = []
        for i in range(k):
            weight = sum(a * b for a, b in zip(ortho[i], columns[k]))
            coeffs.append(weight)
            vector = [a - weight * b for a, b in zip(vector, ortho[i])]
        length = jnp.sqrt(sum(a * a for a in vector))
        coeffs.append(length)
        upper.append(coeffs)
        ortho.append([a / length for a in vector])
    result = [None] * len(columns)
    for k in reversed(range(len(columns))):
        value = ortho[k][0] * beta
        for i in range(k + 1, len(columns)):
            value = value - upper[i][k] * result[i]
        result[k] = value / upper[k][k]
    return result


def combine(gram):
    size = ITERS + 1
    full = [[gram[min(i, j)][max(i, j)] for j in range(size)] for i in range(size)]
    zero = jnp.zeros_like(full[0][0])

    def inner(a, b):
        return sum(
            a[i] * sum(full[i][j] * b[j] for j in range(size) if b[j] is not None)
            for i in range(size)
            if a[i] is not None
        )

    beta = jnp.sqrt(full[0][0])
    vectors = [[1.0 / beta] + [None] * ITERS]
    columns = []
    for step in range(ITERS):
        image = [None] + vectors[step][:ITERS]
        square = inner(image, image)
        dots = [inner(vec, image) for vec in vectors]
        heights = sum(d * d for d in dots)
        height = jnp.sqrt(jnp.maximum(square - heights, 0.001 * square))
        columns.append(dots + [height] + [zero] * (ITERS - step - 1))
        rest = []
        for m in range(size):
            terms = [(dots[i], vectors[i][m]) for i in range(step + 1) if vectors[i][m] is not None]
            if image[m] is None and not terms:
                rest.append(None)
                continue
            value = zero if image[m] is None else image[m]
            for dot, factor in terms:
                value = value - dot * factor
            rest.append(value / height)
        vectors.append(rest)
    weights = least_squares(columns, beta)
    return [
        sum(weights[i] * vectors[i][m] for i in range(ITERS) if vectors[i][m] is not None)
        for m in range(ITERS)
    ]


def local_part(field, blocks, pattern, diagonal):
    count, rows = field.shape
    nblocks = pattern.shape[0]
    picked = field.reshape(count, nblocks, rows // nblocks)[:, pattern]
    local = jnp.einsum("bkoi,nbki->nbo", blocks, picked, precision=HIGH).reshape(count, rows)
    return diagonal[None, :] * field + local


def exchange(field, margin, core):
    count, rows = field.shape
    rims = field.reshape(count, rows // 128, 128)[:, margin].reshape(count, 4, -1)
    groups = lax.axis_size("grp")
    subs = lax.axis_size(SUB)
    up = [(i, i + 1) for i in range(groups - 1)]
    down = [(j, i) for i, j in up]
    across = [(i, ((i + 1) ^ 1) - 1) for i in range(1, subs - 1)]
    from_low = lax.ppermute(rims[:, 1], "grp", up)
    from_high = lax.ppermute(rims[:, 0], "grp", down)
    first = core == 0
    other = lax.ppermute(jnp.where(first, rims[:, 2], rims[:, 3]), SUB, across)
    both = lax.all_gather(jnp.where(first, rims[:, 3], rims[:, 2]), "core")
    partner = jnp.where(first, both[1], both[0])
    sub_low = jnp.where(first, other, partner)
    sub_high = jnp.where(first, partner, other)
    received = jnp.stack([from_low, from_high, sub_low, sub_high], axis=1)
    zeros = jnp.zeros((count, rows // 128, 128), jnp.float32)
    coupled = zeros.at[:, margin.reshape(-1)].add(received.reshape(count, -1, 128))
    return coupled.reshape(count, rows)


def per_device(rhs, diagonal, blocks, pattern, margin, basis, coarse_inverse):
    source = rhs[0, 0]
    diag_row = diagonal[0, 0]
    local_blocks = blocks[0, 0]
    local_pattern = pattern[0, 0]
    local_margin = margin[0, 0]
    local_basis = basis[0, 0]
    inverse_rows = coarse_inverse[0]
    core = lax.axis_index("core")
    krylov = [source]
    conditioned = []
    for _ in range(ITERS):
        field = krylov[-1]
        piece = lax.dot_general(field, local_basis, (((1,), (1,)), ((), ())), precision=HIGH)
        answer = lax.dot_general(
            gather_coarse(piece), inverse_rows, (((1,), (1,)), ((), ())), precision=HIGH
        )
        pre = field / diag_row[None, :] + jnp.dot(answer, local_basis, precision=HIGH)
        conditioned.append(pre)
        base = local_part(pre, local_blocks, local_pattern, diag_row)
        krylov.append(base - exchange(pre, local_margin, core))
    pairs = [(i, j) for j in range(ITERS + 1) for i in range(j + 1)]
    sums = total(jnp.stack([jnp.sum(krylov[i] * krylov[j], axis=-1) for i, j in pairs]))
    gram = [[None] * (ITERS + 1) for _ in range(ITERS + 1)]
    for at, (i, j) in enumerate(pairs):
        gram[i][j] = sums[at]
    factors = combine(gram)
    result = sum(f[:, None] * p for f, p in zip(factors, conditioned))
    return result[None, None]


def solution(mesh):
    groups = mesh.shape["grp"]
    split = Mesh(mesh.devices.reshape(groups, -1, 4, 2), ("grp",) + SUB)
    specs = (
        P("grp", SUB, None, None),
        P("grp", SUB, None),
        P("grp", SUB, None, None, None, None),
        P("grp", SUB, None, None),
        P("grp", SUB, None, None),
        P("grp", SUB, None, None),
        P("grp", SUB, None),
    )
    return jax.shard_map(
        per_device, mesh=split, in_specs=specs, out_specs=P("grp", SUB, None, None), check_vma=False
    )
```

```python
import functools

import jax
import jax.numpy as jnp
from jax import lax
from jax.experimental import pallas as pl
from jax.experimental.pallas import tpu as pltpu
from jax.sharding import Mesh, PartitionSpec as P

ITERS = 3
SUB = ("z", "x", "core")
SHRINK = 1.0 / 256.0
F32 = jnp.float32
BF16 = jnp.bfloat16
HALF = 64
LANES = 128


def vmem():
    return pl.BlockSpec(memory_space=pltpu.VMEM)


def smem():
    return pl.BlockSpec(memory_space=pltpu.SMEM)


def call(body, outs, specs, flops, nbytes, scratch=()):
    return pl.pallas_call(
        body,
        out_shape=outs,
        in_specs=specs,
        out_specs=jax.tree.map(lambda _: vmem(), outs),
        scratch_shapes=scratch,
        compiler_params=pltpu.CompilerParams(vmem_limit_bytes=40 * 1024 * 1024),
        cost_estimate=pl.CostEstimate(flops=flops, bytes_accessed=nbytes, transcendentals=0),
    )


def halves(value):
    high = value.astype(BF16).astype(F32)
    return high, value - high


def stacked(value):
    high, low = halves(value)
    return jnp.concatenate([high, low], axis=0).astype(BF16)


def lane_of(shape):
    return lax.broadcasted_iota(jnp.int32, shape, len(shape) - 1)


def coarse_piece(field, basis_t, core):
    count = field.shape[0]
    out = jnp.dot(stacked(field), basis_t, preferred_element_type=F32)
    lane = lane_of((count, LANES))
    part = out[:count] + jnp.where(lane < HALF, out[count:], 0.0)
    both = part + pltpu.roll(part, HALF, 1)
    start = core * HALF
    return jnp.where((lane >= start) & (lane < start + 48), both, 0.0)


def transposed_halves(value):
    high, low = halves(value)
    rows, width = value.shape
    parts = [high, low]
    if rows < HALF:
        pad = jnp.zeros((HALF - rows, width), F32)
        parts = [high, pad, low, pad]
    return jnp.concatenate(parts, axis=0).T.astype(BF16)


def start_kernel(core_ref, rhs_ref, basis_ref, diag_ref, basis_t_ref, basis_h_ref, inv_ref, piece_ref):
    rows = basis_ref.shape[1]
    for t in range(rows // LANES):
        cols = slice(t * LANES, (t + 1) * LANES)
        basis_t_ref[cols, :] = transposed_halves(basis_ref[:, cols])
    high, low = halves(basis_ref[...])
    basis_h_ref[:, :rows] = high.astype(BF16)
    basis_h_ref[:, rows:] = low.astype(BF16)
    inv_ref[...] = 1.0 / diag_ref[...]
    piece = coarse_piece(rhs_ref[...], basis_t_ref[...], core_ref[0])
    for z in range(piece_ref.shape[0]):
        piece_ref[z] = piece


def coarse_kernel(inverse_ref, out_ref):
    gen, total = inverse_ref.shape
    zero = jnp.zeros((HALF - gen, LANES), BF16)
    for t in range(total // (2 * gen)):
        part = transposed_halves(inverse_ref[:, t * 2 * gen : (t + 1) * 2 * gen])
        row = t * LANES
        out_ref[row : row + gen, :] = part[:gen]
        out_ref[row + gen : row + HALF, :] = zero
        out_ref[row + HALF : row + HALF + gen, :] = part[gen:]
        out_ref[row + HALF + gen : row + LANES, :] = zero


def block_kernel(blocks_ref, out_ref):
    nblocks, knz, blk, _ = blocks_ref.shape
    zero = jnp.zeros((blk, LANES), BF16)

    def step(b, carry):
        for odd in range(2):
            at = 2 * b + odd
            for k in range(knz):
                high, low = halves(blocks_ref[at, k])
                pair = [low, high] if odd else [high, low]
                out_ref[at, k * blk : (k + 1) * blk, :] = (
                    jnp.concatenate(pair, axis=0).T.astype(BF16)
                )
            out_ref[at, knz * blk :, :] = zero
        return carry

    lax.fori_loop(0, nblocks // 2, step, 0)


def field_kernel(
    core_ref, margin_ref, pieces_ref, k_ref, inv_ref, coarse_ref, basis_h_ref,
    p_ref, up_ref, down_ref, across_ref, partner_ref, packed_ref,
):
    count, rows = k_ref.shape
    _, xs, zs, _, _ = pieces_ref.shape
    for z in range(zs):
        for x in range(xs):
            t = z * xs + x
            packed_ref[:, t * LANES : (t + 1) * LANES] = stacked(
                pieces_ref[0, x, z] + pieces_ref[1, x, z]
            )
    out = jnp.dot(packed_ref[...], coarse_ref[...], preferred_element_type=F32)
    part = out[:count] + jnp.where(lane_of((count, LANES)) < HALF, out[count:], 0.0)
    answer = part + pltpu.roll(part, HALF, 1)
    back = jnp.dot(stacked(answer[:, :48]), basis_h_ref[...], preferred_element_type=F32)
    p_ref[...] = (
        k_ref[...] * inv_ref[...] + (back[:count, :rows] + back[count:, :rows]) + back[:count, rows:]
    )
    core = core_ref[0]
    for rim_ref, d in ((up_ref, 1), (down_ref, 0), (across_ref, 2 + core), (partner_ref, 3 - core)):
        for j in range(margin_ref.shape[1]):
            tile = margin_ref[d, j]
            rim_ref[:, j * LANES : (j + 1) * LANES] = p_ref[
                :, pl.ds(pl.multiple_of(tile * LANES, LANES), LANES)
            ]


def local_kernel(pattern_ref, p_ref, diag_ref, weights_ref, out_ref, left_ref, right_ref):
    count, rows = p_ref.shape
    lane = lane_of((2 * count, LANES))
    low_half = lane < HALF
    for t in range(rows // LANES):
        tile = p_ref[:, t * LANES : (t + 1) * LANES]
        high, low = halves(tile)
        both = jnp.concatenate([high, low], axis=0)
        turned = pltpu.roll(both, HALF, 1)
        left_ref[2 * t] = jnp.where(low_half, both, 0.0).astype(BF16)
        left_ref[2 * t + 1] = jnp.where(low_half, turned, 0.0).astype(BF16)
        right_ref[2 * t] = jnp.where(low_half, 0.0, turned).astype(BF16)
        right_ref[2 * t + 1] = jnp.where(low_half, 0.0, both).astype(BF16)
    lower = lane_of((count, LANES)) < HALF

    def product(b):
        first = left_ref[pattern_ref[b, 0]] + right_ref[pattern_ref[b, 1]]
        x = jnp.concatenate([first, left_ref[pattern_ref[b, 2]]], axis=1)
        return jnp.dot(x, weights_ref[b], preferred_element_type=F32)

    for t in range(rows // LANES):
        cols = slice(t * LANES, (t + 1) * LANES)
        even, odd = product(2 * t), product(2 * t + 1)
        even = even[:count] + jnp.where(lower, even[count:], 0.0)
        odd = odd[:count] + jnp.where(lower, 0.0, odd[count:])
        local = jnp.where(lower, even, odd) + pltpu.roll(jnp.where(lower, odd, even), HALF, 1)
        out_ref[:, cols] = diag_ref[:, cols] * p_ref[:, cols] + local


def couple(core_ref, margin_ref, base_ref, low_ref, high_ref, across_ref, both_ref, k_ref):
    core = core_ref[0]
    k_ref[...] = base_ref[...]
    for d, source in ((0, low_ref), (1, high_ref), (2 + core, across_ref), (3 - core, both_ref.at[1 - core])):
        for j in range(margin_ref.shape[1]):
            at = pl.ds(pl.multiple_of(margin_ref[d, j] * LANES, LANES), LANES)
            k_ref[:, at] = k_ref[:, at] - source[:, j * LANES : (j + 1) * LANES]
    k_ref[...] = k_ref[...] * SHRINK


def next_kernel(
    core_ref, margin_ref, base_ref, low_ref, high_ref, across_ref, both_ref, basis_t_ref,
    k_ref, piece_ref,
):
    couple(core_ref, margin_ref, base_ref, low_ref, high_ref, across_ref, both_ref, k_ref)
    piece = coarse_piece(k_ref[...], basis_t_ref[...], core_ref[0])
    for z in range(piece_ref.shape[0]):
        piece_ref[z] = piece


def gram_kernel(
    core_ref, margin_ref, base_ref, low_ref, high_ref, across_ref, both_ref, k0_ref, k1_ref, k2_ref,
    sums_ref, k3_ref,
):
    couple(core_ref, margin_ref, base_ref, low_ref, high_ref, across_ref, both_ref, k3_ref)
    fields = [k0_ref[...], k1_ref[...], k2_ref[...], k3_ref[...]]
    count = fields[0].shape[0]
    lane = lane_of((count, LANES))
    sums = jnp.zeros((count, LANES), F32)
    for at, (i, j) in enumerate(PAIRS):
        sums = jnp.where(lane == at, jnp.sum(fields[i] * fields[j], axis=1, keepdims=True), sums)
    for n in range(sums_ref.shape[0]):
        sums_ref[n] = sums


PAIRS = [(i, j) for j in range(ITERS + 1) for i in range(j + 1)]


def spread(value, axis):
    return lax.all_to_all(value, axis, 0, 0)


def repeated(value, axis):
    return jnp.broadcast_to(value[None], (lax.axis_size(axis),) + value.shape)


def gather_coarse(piece):
    column = spread(piece, "z")
    return lax.all_gather(spread(repeated(column, "x"), "x"), "core")


def total(values):
    part = jnp.sum(spread(values, ("x", "core")), axis=0)
    part = jnp.sum(spread(repeated(part, "z"), "z"), axis=0)
    return jnp.sum(spread(repeated(part, "grp"), "grp"), axis=0)


def least_squares(columns, beta):
    ortho = []
    upper = []
    for k in range(len(columns)):
        vector = columns[k]
        coeffs = []
        for i in range(k):
            weight = sum(a * b for a, b in zip(ortho[i], columns[k]))
            coeffs.append(weight)
            vector = [a - weight * b for a, b in zip(vector, ortho[i])]
        length = jnp.sqrt(sum(a * a for a in vector))
        coeffs.append(length)
        upper.append(coeffs)
        ortho.append([a / length for a in vector])
    result = [None] * len(columns)
    for k in reversed(range(len(columns))):
        value = ortho[k][0] * beta
        for i in range(k + 1, len(columns)):
            value = value - upper[i][k] * result[i]
        result[k] = value / upper[k][k]
    return result


def combine(gram):
    size = ITERS + 1
    full = [[gram[min(i, j)][max(i, j)] for j in range(size)] for i in range(size)]
    zero = jnp.zeros_like(full[0][0])

    def inner(a, b):
        return sum(
            a[i] * sum(full[i][j] * b[j] for j in range(size) if b[j] is not None)
            for i in range(size)
            if a[i] is not None
        )

    beta = jnp.sqrt(full[0][0])
    vectors = [[1.0 / beta] + [None] * ITERS]
    columns = []
    for step in range(ITERS):
        image = [None] + [None if c is None else c * (1.0 / SHRINK) for c in vectors[step][:ITERS]]
        square = inner(image, image)
        dots = [inner(vec, image) for vec in vectors]
        heights = sum(d * d for d in dots)
        height = jnp.sqrt(jnp.maximum(square - heights, 0.001 * square))
        columns.append(dots + [height] + [zero] * (ITERS - step - 1))
        rest = []
        for m in range(size):
            terms = [(dots[i], vectors[i][m]) for i in range(step + 1) if vectors[i][m] is not None]
            if image[m] is None and not terms:
                rest.append(None)
                continue
            value = zero if image[m] is None else image[m]
            for dot, factor in terms:
                value = value - dot * factor
            rest.append(value / height)
        vectors.append(rest)
    weights = least_squares(columns, beta)
    return [
        sum(weights[i] * vectors[i][m] for i in range(ITERS) if vectors[i][m] is not None)
        for m in range(ITERS)
    ]


def shape(*dims, dtype=F32):
    return jax.ShapeDtypeStruct(dims, dtype)


def per_device(rhs, diagonal, blocks, pattern, margin, basis, coarse_inverse):
    source = rhs[0, 0]
    diag_row = diagonal[0]
    pattern = pattern[0, 0]
    margin = margin[0, 0]
    basis = basis[0, 0]
    inverse = coarse_inverse[0]
    count, rows = source.shape
    gen = basis.shape[0]
    nblocks, knz = pattern.shape
    groups, zs, xs = lax.axis_size("grp"), lax.axis_size("z"), lax.axis_size("x")
    subs = lax.axis_size(SUB)
    rim = margin.shape[1] * LANES
    core = lax.axis_index("core").astype(jnp.int32).reshape(1)
    up = [(i, i + 1) for i in range(groups - 1)]
    down = [(j, i) for i, j in up]
    across = [(i, ((i + 1) ^ 1) - 1) for i in range(1, subs - 1)]
    wide = subs * HALF

    basis_t, basis_h, inv_row, piece = call(
        start_kernel,
        [shape(rows, LANES, dtype=BF16), shape(gen, 2 * rows, dtype=BF16), shape(1, rows), shape(zs, count, LANES)],
        [smem(), vmem(), vmem(), vmem()],
        3_000_000,
        1_500_000,
    )(core, source, basis, diag_row)
    coarse = call(coarse_kernel, shape(wide, LANES, dtype=BF16), [vmem()], 1_000_000, 3_200_000)(inverse)
    weights = call(
        block_kernel, shape(nblocks, 4 * HALF, LANES, dtype=BF16), [vmem()], 1_000_000, 5_000_000
    )(blocks[0, 0])

    krylov = [source]
    conditioned = []
    sums = None
    for step in range(ITERS):
        pieces = gather_coarse(piece)
        p, send_up, send_down, send_across, send_partner = call(
            field_kernel,
            [shape(count, rows)] + [shape(count, rim)] * 4,
            [smem(), smem()] + [vmem()] * 5,
            8_000_000,
            3_500_000,
            [pltpu.VMEM((2 * count, wide), BF16)],
        )(core, margin, pieces, krylov[-1], inv_row, coarse, basis_h)
        conditioned.append(p)
        from_low = lax.ppermute(send_up, "grp", up)
        from_high = lax.ppermute(send_down, "grp", down)
        other = lax.ppermute(send_across, SUB, across)
        partner = lax.all_gather(send_partner, "core")
        base = call(
            local_kernel,
            shape(count, rows),
            [smem()] + [vmem()] * 3,
            20_000_000,
            2_500_000,
            [pltpu.VMEM((nblocks, 2 * count, LANES), BF16)] * 2,
        )(pattern, p, diag_row, weights)
        shared = (core, margin, base, from_low, from_high, other, partner)
        if step < ITERS - 1:
            field, piece = call(
                next_kernel,
                [shape(count, rows), shape(zs, count, LANES)],
                [smem(), smem()] + [vmem()] * 6,
                4_000_000,
                1_000_000,
            )(*shared, basis_t)
            krylov.append(field)
        else:
            sums = call(
                gram_kernel,
                shape(2 * xs, count, LANES),
                [smem(), smem()] + [vmem()] * 8,
                400_000,
                500_000,
                [pltpu.VMEM((count, rows), F32)],
            )(*shared, *krylov)
    sums = total(sums)
    gram = [[None] * (ITERS + 1) for _ in range(ITERS + 1)]
    for at, (i, j) in enumerate(PAIRS):
        gram[i][j] = sums[:, at : at + 1]
    factors = combine(gram)
    result = sum(f * p for f, p in zip(factors, conditioned))
    return result[None, None]


def solution(mesh):
    groups = mesh.shape["grp"]
    split = Mesh(mesh.devices.reshape(groups, -1, 4, 2), ("grp",) + SUB)
    specs = (
        P("grp", SUB, None, None),
        P("grp", SUB, None),
        P("grp", SUB, None, None, None, None),
        P("grp", SUB, None, None),
        P("grp", SUB, None, None),
        P("grp", SUB, None, None),
        P("grp", SUB, None),
    )
    return jax.shard_map(
        per_device, mesh=split, in_specs=specs, out_specs=P("grp", SUB, None, None), check_vma=False
    )
```

```python
import functools

import jax
import jax.numpy as jnp
from jax import lax
from jax.experimental import pallas as pl
from jax.experimental.pallas import tpu as pltpu
from jax.sharding import Mesh, PartitionSpec as P

ITERS = 3
SUB = ("z", "x", "core")
SHRINK = 1.0 / 256.0
F32 = jnp.float32
BF16 = jnp.bfloat16
HALF = 64
LANES = 128


def vmem():
    return pl.BlockSpec(memory_space=pltpu.VMEM)


def smem():
    return pl.BlockSpec(memory_space=pltpu.SMEM)


def call(body, outs, specs, flops, nbytes, scratch=(), grant=16):
    return pl.pallas_call(
        body,
        out_shape=outs,
        in_specs=specs,
        out_specs=jax.tree.map(lambda _: vmem(), outs),
        scratch_shapes=scratch,
        compiler_params=pltpu.CompilerParams(vmem_limit_bytes=grant * 1024 * 1024),
        cost_estimate=pl.CostEstimate(flops=flops, bytes_accessed=nbytes, transcendentals=0),
    )


def halves(value):
    high = value.astype(BF16).astype(F32)
    return high, value - high


def stacked(value):
    high, low = halves(value)
    return jnp.concatenate([high, low], axis=0).astype(BF16)


def lane_of(shape):
    return lax.broadcasted_iota(jnp.int32, shape, len(shape) - 1)


def coarse_piece(field, basis_t, core, gen):
    count = field.shape[0]
    out = jnp.dot(stacked(field), basis_t, preferred_element_type=F32)
    lane = lane_of((count, LANES))
    part = out[:count] + jnp.where(lane < HALF, out[count:], 0.0)
    both = part + pltpu.roll(part, HALF, 1)
    half = count // 2
    lane = lane_of((half, LANES))
    own = (lane < HALF) == (core == 0)
    piece = jnp.where(own, both[:half], both[half:])
    return jnp.where((lane & (HALF - 1)) < gen, piece, 0.0)


def transposed_halves(value):
    high, low = halves(value)
    rows, width = value.shape
    parts = [high, low]
    if rows < HALF:
        pad = jnp.zeros((HALF - rows, width), F32)
        parts = [high, pad, low, pad]
    return jnp.concatenate(parts, axis=0).T.astype(BF16)


def start_kernel(
    core_ref, rhs_hbm, basis_hbm, diag_hbm, basis_t_ref, basis_h_ref, inv_ref, piece_ref,
    rhs_ref, basis_ref, diag_ref, sems,
):
    copies = [
        pltpu.make_async_copy(source, target, sems.at[i])
        for i, (source, target) in enumerate(
            ((basis_hbm, basis_ref), (rhs_hbm, rhs_ref), (diag_hbm, diag_ref))
        )
    ]
    for copy in copies:
        copy.start()
    gen, rows = basis_ref.shape
    copies[0].wait()
    for t in range(rows // LANES):
        cols = slice(t * LANES, (t + 1) * LANES)
        basis_t_ref[cols, :] = transposed_halves(basis_ref[:, cols])
    copies[1].wait()
    piece = coarse_piece(rhs_ref[...], basis_t_ref[...], core_ref[0], gen)
    for t in range(piece_ref.shape[0]):
        piece_ref[t] = piece
    high, low = halves(basis_ref[...])
    basis_h_ref[:, :rows] = high.astype(BF16)
    basis_h_ref[:, rows:] = low.astype(BF16)
    copies[2].wait()
    inv_ref[...] = 1.0 / diag_ref[...]


def coarse_kernel(inverse_ref, out_ref):
    gen, total = inverse_ref.shape
    zero = jnp.zeros((HALF - gen, LANES), BF16)
    for t in range(total // (2 * gen)):
        part = transposed_halves(inverse_ref[:, t * 2 * gen : (t + 1) * 2 * gen])
        row = t * LANES
        out_ref[row : row + gen, :] = part[:gen]
        out_ref[row + gen : row + HALF, :] = zero
        out_ref[row + HALF : row + HALF + gen, :] = part[gen:]
        out_ref[row + HALF + gen : row + LANES, :] = zero


def block_kernel(blocks_ref, out_ref):
    nblocks, knz, blk, _ = blocks_ref.shape
    zero = jnp.zeros((blk, LANES), BF16)

    def step(b, carry):
        for odd in range(2):
            at = 2 * b + odd
            for k in range(knz):
                high, low = halves(blocks_ref[at, k])
                pair = [low, high] if odd else [high, low]
                out_ref[at, k * blk : (k + 1) * blk, :] = (
                    jnp.concatenate(pair, axis=0).T.astype(BF16)
                )
            out_ref[at, knz * blk :, :] = zero
        return carry

    lax.fori_loop(0, nblocks // 2, step, 0)


def prepare_kernel(inverse_ref, blocks_ref, coarse_ref, weights_ref):
    coarse_kernel(inverse_ref, coarse_ref)
    block_kernel(blocks_ref, weights_ref)


def field_kernel(
    core_ref, margin_ref, pieces_ref, k_ref, inv_ref, coarse_ref, basis_h_ref,
    p_ref, up_ref, down_ref, across_ref, partner_ref, packed_ref,
):
    count, rows = k_ref.shape
    gen = basis_h_ref.shape[0]
    lower = lane_of((count // 2, LANES)) < HALF
    for t in range(pieces_ref.shape[1]):
        first, second = pieces_ref[0, t], pieces_ref[1, t]
        tile = jnp.concatenate(
            [
                jnp.where(lower, first, second),
                pltpu.roll(jnp.where(lower, second, first), HALF, 1),
            ],
            axis=0,
        )
        packed_ref[:, t * LANES : (t + 1) * LANES] = stacked(tile)
    out = jnp.dot(packed_ref[...], coarse_ref[...], preferred_element_type=F32)
    part = out[:count] + jnp.where(lane_of((count, LANES)) < HALF, out[count:], 0.0)
    answer = part + pltpu.roll(part, HALF, 1)
    back = jnp.dot(stacked(answer[:, :gen]), basis_h_ref[...], preferred_element_type=F32)
    p_ref[...] = (
        k_ref[...] * inv_ref[...] + (back[:count, :rows] + back[count:, :rows]) + back[:count, rows:]
    )
    core = core_ref[0]
    for rim_ref, d in ((up_ref, 1), (down_ref, 0), (across_ref, 2 + core), (partner_ref, 3 - core)):
        for j in range(margin_ref.shape[1]):
            tile = margin_ref[d, j]
            rim_ref[:, j * LANES : (j + 1) * LANES] = p_ref[
                :, pl.ds(pl.multiple_of(tile * LANES, LANES), LANES)
            ]


def local_kernel(pattern_ref, p_ref, diag_ref, weights_ref, out_ref, left_ref, right_ref):
    count, rows = p_ref.shape
    lane = lane_of((2 * count, LANES))
    low_half = lane < HALF
    for t in range(rows // LANES):
        tile = p_ref[:, t * LANES : (t + 1) * LANES]
        high, low = halves(tile)
        both = jnp.concatenate([high, low], axis=0)
        turned = pltpu.roll(both, HALF, 1)
        left_ref[2 * t] = jnp.where(low_half, both, 0.0).astype(BF16)
        left_ref[2 * t + 1] = jnp.where(low_half, turned, 0.0).astype(BF16)
        right_ref[2 * t] = jnp.where(low_half, 0.0, turned).astype(BF16)
        right_ref[2 * t + 1] = jnp.where(low_half, 0.0, both).astype(BF16)
    lower = lane_of((count, LANES)) < HALF

    def product(b):
        first = left_ref[pattern_ref[b, 0]] + right_ref[pattern_ref[b, 1]]
        x = jnp.concatenate([first, left_ref[pattern_ref[b, 2]]], axis=1)
        return jnp.dot(x, weights_ref[b], preferred_element_type=F32)

    for t in range(rows // LANES):
        cols = slice(t * LANES, (t + 1) * LANES)
        even, odd = product(2 * t), product(2 * t + 1)
        even = even[:count] + jnp.where(lower, even[count:], 0.0)
        odd = odd[:count] + jnp.where(lower, 0.0, odd[count:])
        local = jnp.where(lower, even, odd) + pltpu.roll(jnp.where(lower, odd, even), HALF, 1)
        out_ref[:, cols] = diag_ref[:, cols] * p_ref[:, cols] + local


def couple(core_ref, margin_ref, base_ref, low_ref, high_ref, across_ref, partner_ref, k_ref):
    core = core_ref[0]
    k_ref[...] = base_ref[...]
    for d, source in ((0, low_ref), (1, high_ref), (2 + core, across_ref), (3 - core, partner_ref)):
        for j in range(margin_ref.shape[1]):
            at = pl.ds(pl.multiple_of(margin_ref[d, j] * LANES, LANES), LANES)
            k_ref[:, at] = k_ref[:, at] - source[:, j * LANES : (j + 1) * LANES]
    k_ref[...] = k_ref[...] * SHRINK


def next_kernel(
    gen, core_ref, margin_ref, base_ref, low_ref, high_ref, across_ref, partner_ref, basis_t_ref,
    k_ref, piece_ref,
):
    couple(core_ref, margin_ref, base_ref, low_ref, high_ref, across_ref, partner_ref, k_ref)
    piece = coarse_piece(k_ref[...], basis_t_ref[...], core_ref[0], gen)
    for t in range(piece_ref.shape[0]):
        piece_ref[t] = piece


def gram_kernel(
    core_ref, margin_ref, base_ref, low_ref, high_ref, across_ref, partner_ref, k0_ref, k1_ref, k2_ref,
    sums_ref, k3_ref,
):
    couple(core_ref, margin_ref, base_ref, low_ref, high_ref, across_ref, partner_ref, k3_ref)
    fields = [k0_ref[...], k1_ref[...], k2_ref[...], k3_ref[...]]
    count = fields[0].shape[0]
    lane = lane_of((count, LANES))
    place = lane - SLOTS * lax.broadcasted_iota(jnp.int32, (count, LANES), 0)
    sums = jnp.zeros((count, LANES), F32)
    for at, (i, j) in enumerate(PAIRS):
        sums = jnp.where(place == at, jnp.sum(fields[i] * fields[j], axis=1, keepdims=True), sums)
    sums = jnp.sum(sums, axis=0, keepdims=True)
    for n in range(sums_ref.shape[0]):
        sums_ref[n] = sums


def finish_kernel(sums_ref, p0_ref, p1_ref, p2_ref, out_ref):
    count = p0_ref.shape[0]
    sums = jnp.broadcast_to(jnp.sum(sums_ref[...], axis=0), (count, LANES))
    row = lax.broadcasted_iota(jnp.int32, (count, LANES), 0)
    place = lane_of((count, LANES)) - SLOTS * row
    gram = [[None] * (ITERS + 1) for _ in range(ITERS + 1)]
    for at, (i, j) in enumerate(PAIRS):
        gram[i][j] = jnp.sum(jnp.where(place == at, sums, 0.0), axis=1, keepdims=True)
    first, second, third = combine(gram)
    out_ref[...] = first * p0_ref[...] + second * p1_ref[...] + third * p2_ref[...]


SLOTS = 16
PAIRS = [(i, j) for j in range(ITERS + 1) for i in range(j + 1)]


def spread(value, axis):
    return lax.all_to_all(value, axis, 0, 0)


def repeated(value, axis):
    return jnp.broadcast_to(value[None], (lax.axis_size(axis),) + value.shape)


def total(values):
    part = jnp.sum(spread(values, ("z", "x")), axis=0)
    return spread(repeated(part, ("grp", "core")), ("grp", "core"))


def least_squares(columns, beta):
    ortho = []
    upper = []
    for k in range(len(columns)):
        vector = columns[k]
        coeffs = []
        for i in range(k):
            weight = sum(a * b for a, b in zip(ortho[i], columns[k]))
            coeffs.append(weight)
            vector = [a - weight * b for a, b in zip(vector, ortho[i])]
        length = jnp.sqrt(sum(a * a for a in vector))
        coeffs.append(length)
        upper.append(coeffs)
        ortho.append([a / length for a in vector])
    result = [None] * len(columns)
    for k in reversed(range(len(columns))):
        value = ortho[k][0] * beta
        for i in range(k + 1, len(columns)):
            value = value - upper[i][k] * result[i]
        result[k] = value / upper[k][k]
    return result


def combine(gram):
    size = ITERS + 1
    full = [[gram[min(i, j)][max(i, j)] for j in range(size)] for i in range(size)]
    zero = jnp.zeros_like(full[0][0])

    def inner(a, b):
        return sum(
            a[i] * sum(full[i][j] * b[j] for j in range(size) if b[j] is not None)
            for i in range(size)
            if a[i] is not None
        )

    beta = jnp.sqrt(full[0][0])
    vectors = [[1.0 / beta] + [None] * ITERS]
    columns = []
    for step in range(ITERS):
        image = [None] + [None if c is None else c * (1.0 / SHRINK) for c in vectors[step][:ITERS]]
        square = inner(image, image)
        dots = [inner(vec, image) for vec in vectors]
        heights = sum(d * d for d in dots)
        height = jnp.sqrt(jnp.maximum(square - heights, 0.001 * square))
        columns.append(dots + [height] + [zero] * (ITERS - step - 1))
        rest = []
        for m in range(size):
            terms = [(dots[i], vectors[i][m]) for i in range(step + 1) if vectors[i][m] is not None]
            if image[m] is None and not terms:
                rest.append(None)
                continue
            value = zero if image[m] is None else image[m]
            for dot, factor in terms:
                value = value - dot * factor
            rest.append(value / height)
        vectors.append(rest)
    weights = least_squares(columns, beta)
    return [
        sum(weights[i] * vectors[i][m] for i in range(ITERS) if vectors[i][m] is not None)
        for m in range(ITERS)
    ]


def shape(*dims, dtype=F32):
    return jax.ShapeDtypeStruct(dims, dtype)


def per_device(rhs, diagonal, blocks, pattern, margin, basis, coarse_inverse):
    source = rhs[0, 0]
    diag_row = diagonal[0]
    pattern = pattern[0, 0]
    margin = margin[0, 0]
    basis = basis[0, 0]
    inverse = coarse_inverse[0]
    count, rows = source.shape
    gen = basis.shape[0]
    nblocks, knz = pattern.shape
    groups, zs, xs = lax.axis_size("grp"), lax.axis_size("z"), lax.axis_size("x")
    subs = lax.axis_size(SUB)
    rim = margin.shape[1] * LANES
    core = lax.axis_index("core").astype(jnp.int32).reshape(1)
    up = [(i, i + 1) for i in range(groups - 1)]
    down = [(j, i) for i, j in up]
    across = [(i, ((i + 1) ^ 1) - 1) for i in range(1, subs - 1)]
    wide = subs * HALF

    chips = zs * xs
    anywhere = pl.BlockSpec(memory_space=pl.ANY)

    basis_t, basis_h, inv_row, piece = call(
        start_kernel,
        [
            shape(rows, LANES, dtype=BF16),
            shape(gen, 2 * rows, dtype=BF16),
            shape(1, rows),
            shape(chips, count // 2, LANES),
        ],
        [smem(), anywhere, anywhere, anywhere],
        3_000_000,
        1_500_000,
        [
            pltpu.VMEM((count, rows), F32),
            pltpu.VMEM((gen, rows), F32),
            pltpu.VMEM((1, rows), F32),
            pltpu.SemaphoreType.DMA((3,)),
        ],
        60,
    )(core, source, basis, diag_row)
    coarse, weights = call(
        prepare_kernel,
        [shape(wide, LANES, dtype=BF16), shape(nblocks, 4 * HALF, LANES, dtype=BF16)],
        [vmem(), vmem()],
        2_000_000,
        8_000_000,
    )(inverse, blocks[0, 0])

    krylov = [source]
    conditioned = []
    sums = None
    for step in range(ITERS):
        pieces = spread(piece, ("z", "x"))
        if step == 0:
            pieces, coarse, weights = lax.optimization_barrier((pieces, coarse, weights))
        pieces = lax.all_gather(pieces, "core")
        p, send_up, send_down, send_across, send_partner = call(
            field_kernel,
            [shape(count, rows)] + [shape(count, rim)] * 4,
            [smem(), smem()] + [vmem()] * 5,
            8_000_000,
            3_500_000,
            [pltpu.VMEM((2 * count, wide), BF16)],
        )(core, margin, pieces, krylov[-1], inv_row, coarse, basis_h)
        conditioned.append(p)
        from_low = lax.ppermute(send_up, "grp", up)
        from_high = lax.ppermute(send_down, "grp", down)
        other = lax.ppermute(send_across, SUB, across)
        partner = lax.ppermute(send_partner, "core", [(0, 1), (1, 0)])
        base = call(
            local_kernel,
            shape(count, rows),
            [smem()] + [vmem()] * 3,
            20_000_000,
            2_500_000,
            [pltpu.VMEM((nblocks, 2 * count, LANES), BF16)] * 2,
        )(pattern, p, diag_row, weights)
        shared = (core, margin, base, from_low, from_high, other, partner)
        if step < ITERS - 1:
            field, piece = call(
                functools.partial(next_kernel, gen),
                [shape(count, rows), shape(chips, count // 2, LANES)],
                [smem(), smem()] + [vmem()] * 6,
                4_000_000,
                1_000_000,
            )(*shared, basis_t)
            krylov.append(field)
        else:
            sums = call(
                gram_kernel,
                shape(chips, 1, LANES),
                [smem(), smem()] + [vmem()] * 8,
                400_000,
                500_000,
                [pltpu.VMEM((count, rows), F32)],
            )(*shared, *krylov)
    result = call(finish_kernel, shape(count, rows), [vmem()] * 4, 100_000, 300_000)(
        total(sums), *conditioned
    )
    return result[None, None]


def solution(mesh):
    groups = mesh.shape["grp"]
    split = Mesh(mesh.devices.reshape(groups, -1, 4, 2), ("grp",) + SUB)
    specs = (
        P("grp", SUB, None, None),
        P("grp", SUB, None),
        P("grp", SUB, None, None, None, None),
        P("grp", SUB, None, None),
        P("grp", SUB, None, None),
        P("grp", SUB, None, None),
        P("grp", SUB, None),
    )
    return jax.shard_map(
        per_device, mesh=split, in_specs=specs, out_specs=P("grp", SUB, None, None), check_vma=False
    )
```

```python
import functools

import jax
import jax.numpy as jnp
from jax import lax
from jax.experimental import pallas as pl
from jax.experimental.pallas import tpu as pltpu
from jax.sharding import Mesh, PartitionSpec as P

ITERS = 3
SUB = ("z", "x", "core")
SHRINK = 1.0 / 256.0
F32 = jnp.float32
BF16 = jnp.bfloat16
HALF = 64
LANES = 128


def vmem():
    return pl.BlockSpec(memory_space=pltpu.VMEM)


def smem():
    return pl.BlockSpec(memory_space=pltpu.SMEM)


def call(body, outs, specs, flops, nbytes, scratch=(), grant=16):
    return pl.pallas_call(
        body,
        out_shape=outs,
        in_specs=specs,
        out_specs=jax.tree.map(lambda _: vmem(), outs),
        scratch_shapes=scratch,
        compiler_params=pltpu.CompilerParams(vmem_limit_bytes=grant * 1024 * 1024),
        cost_estimate=pl.CostEstimate(flops=flops, bytes_accessed=nbytes, transcendentals=0),
    )


def halves(value):
    high = value.astype(BF16).astype(F32)
    return high, value - high


def stacked(value):
    high, low = halves(value)
    return jnp.concatenate([high, low], axis=0).astype(BF16)


def lane_of(shape):
    return lax.broadcasted_iota(jnp.int32, shape, len(shape) - 1)


def coarse_piece(field, basis_t, core, gen):
    count = field.shape[0]
    out = jnp.dot(stacked(field), basis_t, preferred_element_type=F32)
    lane = lane_of((count, LANES))
    part = out[:count] + jnp.where(lane < HALF, out[count:], 0.0)
    both = part + pltpu.roll(part, HALF, 1)
    half = count // 2
    lane = lane_of((half, LANES))
    own = (lane < HALF) == (core == 0)
    piece = jnp.where(own, both[:half], both[half:])
    return jnp.where((lane & (HALF - 1)) < gen, piece, 0.0)


def transposed_halves(value):
    high, low = halves(value)
    rows, width = value.shape
    parts = [high, low]
    if rows < HALF:
        pad = jnp.zeros((HALF - rows, width), F32)
        parts = [high, pad, low, pad]
    return jnp.concatenate(parts, axis=0).T.astype(BF16)


def start_kernel(core_ref, rhs_hbm, basis_hbm, piece_ref, rhs_ref, basis_ref, sems):
    copies = [
        pltpu.make_async_copy(source, target, sems.at[i])
        for i, (source, target) in enumerate(((basis_hbm, basis_ref), (rhs_hbm, rhs_ref)))
    ]
    for copy in copies:
        copy.start()
    for copy in copies:
        copy.wait()
    gen, rows = basis_ref.shape
    basis_t = jnp.concatenate(
        [
            transposed_halves(basis_ref[:, t * LANES : (t + 1) * LANES])
            for t in range(rows // LANES)
        ],
        axis=0,
    )
    piece = coarse_piece(rhs_ref[...], basis_t, core_ref[0], gen)
    for t in range(piece_ref.shape[0]):
        piece_ref[t] = piece


def prepare_kernel(basis_ref, diag_ref, blocks_ref, basis_t_ref, basis_h_ref, inv_ref, weights_ref):
    rows = basis_ref.shape[1]
    for t in range(rows // LANES):
        cols = slice(t * LANES, (t + 1) * LANES)
        basis_t_ref[cols, :] = transposed_halves(basis_ref[:, cols])
    high, low = halves(basis_ref[...])
    basis_h_ref[:, :rows] = high.astype(BF16)
    basis_h_ref[:, rows:] = low.astype(BF16)
    inv_ref[...] = 1.0 / diag_ref[...]
    block_kernel(blocks_ref, weights_ref)


def coarse_kernel(after_ref, inverse_ref, out_ref):
    gen, total = inverse_ref.shape
    zero = jnp.zeros((HALF - gen, LANES), BF16)
    for t in range(total // (2 * gen)):
        part = transposed_halves(inverse_ref[:, t * 2 * gen : (t + 1) * 2 * gen])
        row = t * LANES
        out_ref[row : row + gen, :] = part[:gen]
        out_ref[row + gen : row + HALF, :] = zero
        out_ref[row + HALF : row + HALF + gen, :] = part[gen:]
        out_ref[row + HALF + gen : row + LANES, :] = zero


def block_kernel(blocks_ref, out_ref):
    nblocks, knz, blk, _ = blocks_ref.shape
    zero = jnp.zeros((blk, LANES), BF16)

    def step(b, carry):
        for odd in range(2):
            at = 2 * b + odd
            for k in range(knz):
                high, low = halves(blocks_ref[at, k])
                pair = [low, high] if odd else [high, low]
                out_ref[at, k * blk : (k + 1) * blk, :] = (
                    jnp.concatenate(pair, axis=0).T.astype(BF16)
                )
            out_ref[at, knz * blk :, :] = zero
        return carry

    lax.fori_loop(0, nblocks // 2, step, 0)


def field_kernel(
    core_ref, margin_ref, pieces_ref, k_ref, inv_ref, coarse_ref, basis_h_ref,
    p_ref, rims_ref, across_ref, packed_ref,
):
    count, rows = k_ref.shape
    gen = basis_h_ref.shape[0]
    lower = lane_of((count // 2, LANES)) < HALF
    for t in range(pieces_ref.shape[1]):
        first, second = pieces_ref[0, t], pieces_ref[1, t]
        tile = jnp.concatenate(
            [
                jnp.where(lower, first, second),
                pltpu.roll(jnp.where(lower, second, first), HALF, 1),
            ],
            axis=0,
        )
        packed_ref[:, t * LANES : (t + 1) * LANES] = stacked(tile)
    out = jnp.dot(packed_ref[...], coarse_ref[...], preferred_element_type=F32)
    part = out[:count] + jnp.where(lane_of((count, LANES)) < HALF, out[count:], 0.0)
    answer = part + pltpu.roll(part, HALF, 1)
    back = jnp.dot(stacked(answer[:, :gen]), basis_h_ref[...], preferred_element_type=F32)
    p_ref[...] = (
        k_ref[...] * inv_ref[...] + (back[:count, :rows] + back[count:, :rows]) + back[:count, rows:]
    )
    core = core_ref[0]
    for rim_ref, d in (
        (rims_ref.at[0], 1), (rims_ref.at[1], 0), (rims_ref.at[2], 3 - core), (across_ref, 2 + core)
    ):
        for j in range(margin_ref.shape[1]):
            tile = margin_ref[d, j]
            rim_ref[:, j * LANES : (j + 1) * LANES] = p_ref[
                :, pl.ds(pl.multiple_of(tile * LANES, LANES), LANES)
            ]


def local_kernel(pattern_ref, p_ref, diag_ref, weights_ref, out_ref, left_ref, right_ref):
    count, rows = p_ref.shape
    lane = lane_of((2 * count, LANES))
    low_half = lane < HALF
    for t in range(rows // LANES):
        tile = p_ref[:, t * LANES : (t + 1) * LANES]
        high, low = halves(tile)
        both = jnp.concatenate([high, low], axis=0)
        turned = pltpu.roll(both, HALF, 1)
        left_ref[2 * t] = jnp.where(low_half, both, 0.0).astype(BF16)
        left_ref[2 * t + 1] = jnp.where(low_half, turned, 0.0).astype(BF16)
        right_ref[2 * t] = jnp.where(low_half, 0.0, turned).astype(BF16)
        right_ref[2 * t + 1] = jnp.where(low_half, 0.0, both).astype(BF16)
    lower = lane_of((count, LANES)) < HALF

    def product(b):
        first = left_ref[pattern_ref[b, 0]] + right_ref[pattern_ref[b, 1]]
        x = jnp.concatenate([first, left_ref[pattern_ref[b, 2]]], axis=1)
        return jnp.dot(x, weights_ref[b], preferred_element_type=F32)

    for t in range(rows // LANES):
        cols = slice(t * LANES, (t + 1) * LANES)
        even, odd = product(2 * t), product(2 * t + 1)
        even = even[:count] + jnp.where(lower, even[count:], 0.0)
        odd = odd[:count] + jnp.where(lower, 0.0, odd[count:])
        local = jnp.where(lower, even, odd) + pltpu.roll(jnp.where(lower, odd, even), HALF, 1)
        out_ref[:, cols] = diag_ref[:, cols] * p_ref[:, cols] + local


def couple(core_ref, margin_ref, base_ref, vertical_ref, across_ref, pair_ref, k_ref):
    core = core_ref[0]
    k_ref[...] = base_ref[...]
    for d, source in (
        (0, vertical_ref.at[0, core]),
        (1, vertical_ref.at[1, core]),
        (2 + core, across_ref),
        (3 - core, pair_ref.at[1 - core, 2]),
    ):
        for j in range(margin_ref.shape[1]):
            at = pl.ds(pl.multiple_of(margin_ref[d, j] * LANES, LANES), LANES)
            k_ref[:, at] = k_ref[:, at] - source[:, j * LANES : (j + 1) * LANES]
    k_ref[...] = k_ref[...] * SHRINK


def next_kernel(
    gen, core_ref, margin_ref, base_ref, vertical_ref, across_ref, pair_ref, basis_t_ref,
    k_ref, piece_ref,
):
    couple(core_ref, margin_ref, base_ref, vertical_ref, across_ref, pair_ref, k_ref)
    piece = coarse_piece(k_ref[...], basis_t_ref[...], core_ref[0], gen)
    for t in range(piece_ref.shape[0]):
        piece_ref[t] = piece


def gram_kernel(
    core_ref, margin_ref, base_ref, vertical_ref, across_ref, pair_ref, k0_ref, k1_ref, k2_ref,
    sums_ref, k3_ref,
):
    couple(core_ref, margin_ref, base_ref, vertical_ref, across_ref, pair_ref, k3_ref)
    fields = [k0_ref[...], k1_ref[...], k2_ref[...], k3_ref[...]]
    count = fields[0].shape[0]
    lane = lane_of((count, LANES))
    place = lane - SLOTS * lax.broadcasted_iota(jnp.int32, (count, LANES), 0)
    sums = jnp.zeros((count, LANES), F32)
    for at, (i, j) in enumerate(PAIRS):
        sums = jnp.where(place == at, jnp.sum(fields[i] * fields[j], axis=1, keepdims=True), sums)
    sums = jnp.sum(sums, axis=0, keepdims=True)
    for n in range(sums_ref.shape[0]):
        sums_ref[n] = sums


def finish_kernel(sums_ref, p0_ref, p1_ref, p2_ref, out_ref):
    count = p0_ref.shape[0]
    sums = jnp.broadcast_to(jnp.sum(sums_ref[...], axis=0), (count, LANES))
    row = lax.broadcasted_iota(jnp.int32, (count, LANES), 0)
    place = lane_of((count, LANES)) - SLOTS * row
    gram = [[None] * (ITERS + 1) for _ in range(ITERS + 1)]
    for at, (i, j) in enumerate(PAIRS):
        gram[i][j] = jnp.sum(jnp.where(place == at, sums, 0.0), axis=1, keepdims=True)
    first, second, third = combine(gram)
    out_ref[...] = first * p0_ref[...] + second * p1_ref[...] + third * p2_ref[...]


SLOTS = 16
PAIRS = [(i, j) for j in range(ITERS + 1) for i in range(j + 1)]


def spread(value, axis):
    return lax.all_to_all(value, axis, 0, 0)


def repeated(value, axis):
    return jnp.broadcast_to(value[None], (lax.axis_size(axis),) + value.shape)


def total(values):
    part = jnp.sum(spread(values, ("z", "x")), axis=0)
    return spread(repeated(part, ("grp", "core")), ("grp", "core"))


def least_squares(columns, beta):
    ortho = []
    upper = []
    for k in range(len(columns)):
        vector = columns[k]
        coeffs = []
        for i in range(k):
            weight = sum(a * b for a, b in zip(ortho[i], columns[k]))
            coeffs.append(weight)
            vector = [a - weight * b for a, b in zip(vector, ortho[i])]
        length = jnp.sqrt(sum(a * a for a in vector))
        coeffs.append(length)
        upper.append(coeffs)
        ortho.append([a / length for a in vector])
    result = [None] * len(columns)
    for k in reversed(range(len(columns))):
        value = ortho[k][0] * beta
        for i in range(k + 1, len(columns)):
            value = value - upper[i][k] * result[i]
        result[k] = value / upper[k][k]
    return result


def combine(gram):
    size = ITERS + 1
    full = [[gram[min(i, j)][max(i, j)] for j in range(size)] for i in range(size)]
    zero = jnp.zeros_like(full[0][0])

    def inner(a, b):
        return sum(
            a[i] * sum(full[i][j] * b[j] for j in range(size) if b[j] is not None)
            for i in range(size)
            if a[i] is not None
        )

    beta = jnp.sqrt(full[0][0])
    vectors = [[1.0 / beta] + [None] * ITERS]
    columns = []
    for step in range(ITERS):
        image = [None] + [None if c is None else c * (1.0 / SHRINK) for c in vectors[step][:ITERS]]
        square = inner(image, image)
        dots = [inner(vec, image) for vec in vectors]
        heights = sum(d * d for d in dots)
        height = jnp.sqrt(jnp.maximum(square - heights, 0.001 * square))
        columns.append(dots + [height] + [zero] * (ITERS - step - 1))
        rest = []
        for m in range(size):
            terms = [(dots[i], vectors[i][m]) for i in range(step + 1) if vectors[i][m] is not None]
            if image[m] is None and not terms:
                rest.append(None)
                continue
            value = zero if image[m] is None else image[m]
            for dot, factor in terms:
                value = value - dot * factor
            rest.append(value / height)
        vectors.append(rest)
    weights = least_squares(columns, beta)
    return [
        sum(weights[i] * vectors[i][m] for i in range(ITERS) if vectors[i][m] is not None)
        for m in range(ITERS)
    ]


def shape(*dims, dtype=F32):
    return jax.ShapeDtypeStruct(dims, dtype)


def per_device(rhs, diagonal, blocks, pattern, margin, basis, coarse_inverse):
    source = rhs[0, 0]
    diag_row = diagonal[0]
    pattern = pattern[0, 0]
    margin = margin[0, 0]
    basis = basis[0, 0]
    inverse = coarse_inverse[0]
    count, rows = source.shape
    gen = basis.shape[0]
    nblocks, knz = pattern.shape
    groups, zs, xs = lax.axis_size("grp"), lax.axis_size("z"), lax.axis_size("x")
    subs = lax.axis_size(SUB)
    rim = margin.shape[1] * LANES
    core = lax.axis_index("core").astype(jnp.int32).reshape(1)
    vertical = [(2 * g, 2 * g + 2) for g in range(groups - 1)]
    vertical += [(2 * g + 3, 2 * g + 1) for g in range(groups - 1)]
    across = [(i, ((i + 1) ^ 1) - 1) for i in range(1, subs - 1)]
    wide = subs * HALF

    chips = zs * xs
    anywhere = pl.BlockSpec(memory_space=pl.ANY)

    piece = call(
        start_kernel,
        shape(chips, count // 2, LANES),
        [smem(), anywhere, anywhere],
        3_000_000,
        1_500_000,
        [
            pltpu.VMEM((count, rows), F32),
            pltpu.VMEM((gen, rows), F32),
            pltpu.SemaphoreType.DMA((2,)),
        ],
        60,
    )(core, source, basis)
    basis_t, basis_h, inv_row, weights = call(
        prepare_kernel,
        [
            shape(rows, LANES, dtype=BF16),
            shape(gen, 2 * rows, dtype=BF16),
            shape(1, rows),
            shape(nblocks, 4 * HALF, LANES, dtype=BF16),
        ],
        [vmem()] * 3,
        2_000_000,
        6_000_000,
    )(basis, diag_row, blocks[0, 0])
    coarse = call(
        coarse_kernel, shape(wide, LANES, dtype=BF16), [anywhere, vmem()], 1_000_000, 3_200_000
    )(inv_row, inverse)

    krylov = [source]
    conditioned = []
    sums = None
    for step in range(ITERS):
        pieces = spread(piece, ("z", "x"))
        if step == 0:
            pieces, weights = lax.optimization_barrier((pieces, weights))
        pieces = lax.all_gather(pieces, "core")
        p, rims, send_across = call(
            field_kernel,
            [shape(count, rows), shape(3, count, rim), shape(count, rim)],
            [smem(), smem()] + [vmem()] * 5,
            8_000_000,
            3_500_000,
            [pltpu.VMEM((2 * count, wide), BF16)],
        )(core, margin, pieces, krylov[-1], inv_row, coarse, basis_h)
        conditioned.append(p)
        other = lax.ppermute(send_across, SUB, across)
        pair = lax.all_gather(rims, "core")
        carried = lax.dynamic_index_in_dim(pair, core[0], axis=1, keepdims=False)
        carried = lax.ppermute(carried, ("grp", "core"), vertical)
        base = call(
            local_kernel,
            shape(count, rows),
            [smem()] + [vmem()] * 3,
            20_000_000,
            2_500_000,
            [pltpu.VMEM((nblocks, 2 * count, LANES), BF16)] * 2,
        )(pattern, p, diag_row, weights)
        shared = (core, margin, base, lax.all_gather(carried, "core"), other, pair)
        if step < ITERS - 1:
            field, piece = call(
                functools.partial(next_kernel, gen),
                [shape(count, rows), shape(chips, count // 2, LANES)],
                [smem(), smem()] + [vmem()] * 5,
                4_000_000,
                1_000_000,
            )(*shared, basis_t)
            krylov.append(field)
        else:
            sums = call(
                gram_kernel,
                shape(chips, 1, LANES),
                [smem(), smem()] + [vmem()] * 7,
                400_000,
                500_000,
                [pltpu.VMEM((count, rows), F32)],
            )(*shared, *krylov)
    result = call(finish_kernel, shape(count, rows), [vmem()] * 4, 100_000, 300_000)(
        total(sums), *conditioned
    )
    return result[None, None]


def solution(mesh):
    groups = mesh.shape["grp"]
    split = Mesh(mesh.devices.reshape(groups, -1, 4, 2), ("grp",) + SUB)
    specs = (
        P("grp", SUB, None, None),
        P("grp", SUB, None),
        P("grp", SUB, None, None, None, None),
        P("grp", SUB, None, None),
        P("grp", SUB, None, None),
        P("grp", SUB, None, None),
        P("grp", SUB, None),
    )
    return jax.shard_map(
        per_device, mesh=split, in_specs=specs, out_specs=P("grp", SUB, None, None), check_vma=False
    )
```

```python
import functools

import jax
import jax.numpy as jnp
from jax import lax
from jax.experimental import pallas as pl
from jax.experimental.pallas import tpu as pltpu
from jax.sharding import Mesh, PartitionSpec as P

ITERS = 3
SUB = ("z", "x", "core")
SHRINK = 1.0 / 256.0
F32 = jnp.float32
BF16 = jnp.bfloat16
HALF = 64
LANES = 128


def vmem():
    return pl.BlockSpec(memory_space=pltpu.VMEM)


def smem():
    return pl.BlockSpec(memory_space=pltpu.SMEM)


def call(body, outs, specs, flops, nbytes, scratch=(), grant=16):
    return pl.pallas_call(
        body,
        out_shape=outs,
        in_specs=specs,
        out_specs=jax.tree.map(lambda _: vmem(), outs),
        scratch_shapes=scratch,
        compiler_params=pltpu.CompilerParams(vmem_limit_bytes=grant * 1024 * 1024),
        cost_estimate=pl.CostEstimate(flops=flops, bytes_accessed=nbytes, transcendentals=0),
    )


def halves(value):
    high = value.astype(BF16).astype(F32)
    return high, value - high


def stacked(value):
    high, low = halves(value)
    return jnp.concatenate([high, low], axis=0).astype(BF16)


def lane_of(shape):
    return lax.broadcasted_iota(jnp.int32, shape, len(shape) - 1)


def coarse_piece(field, basis_t, core, gen):
    count = field.shape[0]
    out = jnp.dot(stacked(field), basis_t, preferred_element_type=F32)
    lane = lane_of((count, LANES))
    part = out[:count] + jnp.where(lane < HALF, out[count:], 0.0)
    both = part + pltpu.roll(part, HALF, 1)
    half = count // 2
    lane = lane_of((half, LANES))
    own = (lane < HALF) == (core == 0)
    piece = jnp.where(own, both[:half], both[half:])
    return jnp.where((lane & (HALF - 1)) < gen, piece, 0.0)


def transposed_halves(value):
    high, low = halves(value)
    rows, width = value.shape
    parts = [high, low]
    if rows < HALF:
        pad = jnp.zeros((HALF - rows, width), F32)
        parts = [high, pad, low, pad]
    return jnp.concatenate(parts, axis=0).T.astype(BF16)


def start_kernel(core_ref, rhs_hbm, basis_hbm, piece_ref, rhs_ref, basis_ref, sems):
    copies = [
        pltpu.make_async_copy(source, target, sems.at[i])
        for i, (source, target) in enumerate(((basis_hbm, basis_ref), (rhs_hbm, rhs_ref)))
    ]
    for copy in copies:
        copy.start()
    for copy in copies:
        copy.wait()
    gen, rows = basis_ref.shape
    basis_t = jnp.concatenate(
        [
            transposed_halves(basis_ref[:, t * LANES : (t + 1) * LANES])
            for t in range(rows // LANES)
        ],
        axis=0,
    )
    piece = coarse_piece(rhs_ref[...], basis_t, core_ref[0], gen)
    for t in range(piece_ref.shape[0]):
        piece_ref[t] = piece


def prepare_kernel(basis_ref, diag_ref, blocks_ref, basis_t_ref, basis_h_ref, inv_ref, weights_ref):
    rows = basis_ref.shape[1]
    for t in range(rows // LANES):
        cols = slice(t * LANES, (t + 1) * LANES)
        basis_t_ref[cols, :] = transposed_halves(basis_ref[:, cols])
    high, low = halves(basis_ref[...])
    basis_h_ref[:, :rows] = high.astype(BF16)
    basis_h_ref[:, rows:] = low.astype(BF16)
    inv_ref[...] = 1.0 / diag_ref[...]
    block_kernel(blocks_ref, weights_ref)


def coarse_kernel(after_ref, inverse_ref, out_ref):
    gen, total = inverse_ref.shape
    zero = jnp.zeros((HALF - gen, LANES), BF16)
    for t in range(total // (2 * gen)):
        part = transposed_halves(inverse_ref[:, t * 2 * gen : (t + 1) * 2 * gen])
        row = t * LANES
        out_ref[row : row + gen, :] = part[:gen]
        out_ref[row + gen : row + HALF, :] = zero
        out_ref[row + HALF : row + HALF + gen, :] = part[gen:]
        out_ref[row + HALF + gen : row + LANES, :] = zero


def block_kernel(blocks_ref, out_ref):
    nblocks, knz, blk, _ = blocks_ref.shape
    zero = jnp.zeros((blk, LANES), BF16)

    def step(b, carry):
        for odd in range(2):
            at = 2 * b + odd
            for k in range(knz):
                high, low = halves(blocks_ref[at, k])
                pair = [low, high] if odd else [high, low]
                out_ref[at, k * blk : (k + 1) * blk, :] = (
                    jnp.concatenate(pair, axis=0).T.astype(BF16)
                )
            out_ref[at, knz * blk :, :] = zero
        return carry

    lax.fori_loop(0, nblocks // 2, step, 0)


def field_kernel(
    core_ref, margin_ref, pieces_ref, k_ref, inv_ref, coarse_ref, basis_h_ref,
    p_ref, rims_ref, across_ref, packed_ref,
):
    count, rows = k_ref.shape
    gen = basis_h_ref.shape[0]
    lower = lane_of((count // 2, LANES)) < HALF
    for t in range(pieces_ref.shape[1]):
        first, second = pieces_ref[0, t], pieces_ref[1, t]
        tile = jnp.concatenate(
            [
                jnp.where(lower, first, second),
                pltpu.roll(jnp.where(lower, second, first), HALF, 1),
            ],
            axis=0,
        )
        packed_ref[:, t * LANES : (t + 1) * LANES] = stacked(tile)
    out = jnp.dot(packed_ref[...], coarse_ref[...], preferred_element_type=F32)
    part = out[:count] + jnp.where(lane_of((count, LANES)) < HALF, out[count:], 0.0)
    answer = part + pltpu.roll(part, HALF, 1)
    back = jnp.dot(stacked(answer[:, :gen]), basis_h_ref[...], preferred_element_type=F32)
    p_ref[...] = (
        k_ref[...] * inv_ref[...] + (back[:count, :rows] + back[count:, :rows]) + back[:count, rows:]
    )
    core = core_ref[0]
    for rim_ref, d in (
        (rims_ref.at[0], 1), (rims_ref.at[1], 0), (rims_ref.at[2], 3 - core), (across_ref, 2 + core)
    ):
        for j in range(margin_ref.shape[1]):
            tile = margin_ref[d, j]
            rim_ref[:, j * LANES : (j + 1) * LANES] = p_ref[
                :, pl.ds(pl.multiple_of(tile * LANES, LANES), LANES)
            ]


def local_kernel(pattern_ref, p_ref, diag_ref, weights_ref, out_ref, left_ref, right_ref):
    count, rows = p_ref.shape
    lane = lane_of((2 * count, LANES))
    low_half = lane < HALF
    for t in range(rows // LANES):
        tile = p_ref[:, t * LANES : (t + 1) * LANES]
        high, low = halves(tile)
        both = jnp.concatenate([high, low], axis=0)
        turned = pltpu.roll(both, HALF, 1)
        left_ref[2 * t] = jnp.where(low_half, both, 0.0).astype(BF16)
        left_ref[2 * t + 1] = jnp.where(low_half, turned, 0.0).astype(BF16)
        right_ref[2 * t] = jnp.where(low_half, 0.0, turned).astype(BF16)
        right_ref[2 * t + 1] = jnp.where(low_half, 0.0, both).astype(BF16)
    lower = lane_of((count, LANES)) < HALF

    def product(b):
        first = left_ref[pattern_ref[b, 0]] + right_ref[pattern_ref[b, 1]]
        x = jnp.concatenate([first, left_ref[pattern_ref[b, 2]]], axis=1)
        return jnp.dot(x, weights_ref[b], preferred_element_type=F32)

    for t in range(rows // LANES):
        cols = slice(t * LANES, (t + 1) * LANES)
        even, odd = product(2 * t), product(2 * t + 1)
        even = even[:count] + jnp.where(lower, even[count:], 0.0)
        odd = odd[:count] + jnp.where(lower, 0.0, odd[count:])
        local = jnp.where(lower, even, odd) + pltpu.roll(jnp.where(lower, odd, even), HALF, 1)
        out_ref[:, cols] = diag_ref[:, cols] * p_ref[:, cols] + local


def couple(core_ref, margin_ref, base_ref, vertical_ref, across_ref, pair_ref, k_ref):
    core = core_ref[0]
    k_ref[...] = base_ref[...]
    for d, source in (
        (0, vertical_ref.at[0, core]),
        (1, vertical_ref.at[1, core]),
        (2 + core, across_ref),
        (3 - core, pair_ref.at[1 - core, 2]),
    ):
        for j in range(margin_ref.shape[1]):
            at = pl.ds(pl.multiple_of(margin_ref[d, j] * LANES, LANES), LANES)
            k_ref[:, at] = k_ref[:, at] - source[:, j * LANES : (j + 1) * LANES]
    k_ref[...] = k_ref[...] * SHRINK


def next_kernel(
    gen, core_ref, margin_ref, base_ref, vertical_ref, across_ref, pair_ref, basis_t_ref,
    k_ref, piece_ref,
):
    couple(core_ref, margin_ref, base_ref, vertical_ref, across_ref, pair_ref, k_ref)
    piece = coarse_piece(k_ref[...], basis_t_ref[...], core_ref[0], gen)
    for t in range(piece_ref.shape[0]):
        piece_ref[t] = piece


def gram_kernel(
    core_ref, margin_ref, base_ref, vertical_ref, across_ref, pair_ref, k0_ref, k1_ref, k2_ref,
    sums_ref, k3_ref,
):
    couple(core_ref, margin_ref, base_ref, vertical_ref, across_ref, pair_ref, k3_ref)
    fields = [k0_ref[...], k1_ref[...], k2_ref[...], k3_ref[...]]
    count = fields[0].shape[0]
    lane = lane_of((count, LANES))
    place = lane - SLOTS * lax.broadcasted_iota(jnp.int32, (count, LANES), 0)
    sums = jnp.zeros((count, LANES), F32)
    for at, (i, j) in enumerate(PAIRS):
        sums = jnp.where(place == at, jnp.sum(fields[i] * fields[j], axis=1, keepdims=True), sums)
    sums = jnp.sum(sums, axis=0, keepdims=True)
    for n in range(sums_ref.shape[0]):
        sums_ref[n] = sums


def finish_kernel(sums_ref, p0_ref, p1_ref, p2_ref, out_ref):
    count = p0_ref.shape[0]
    sums = jnp.broadcast_to(jnp.sum(sums_ref[...], axis=0), (count, LANES))
    row = lax.broadcasted_iota(jnp.int32, (count, LANES), 0)
    place = lane_of((count, LANES)) - SLOTS * row
    gram = [[None] * (ITERS + 1) for _ in range(ITERS + 1)]
    for at, (i, j) in enumerate(PAIRS):
        gram[i][j] = jnp.sum(jnp.where(place == at, sums, 0.0), axis=1, keepdims=True)
    first, second, third = combine(gram)
    out_ref[...] = first * p0_ref[...] + second * p1_ref[...] + third * p2_ref[...]


SLOTS = 16
PAIRS = [(i, j) for j in range(ITERS + 1) for i in range(j + 1)]


def spread(value, axis):
    return lax.all_to_all(value, axis, 0, 0)


def repeated(value, axis):
    return jnp.broadcast_to(value[None], (lax.axis_size(axis),) + value.shape)


def total(values):
    part = jnp.sum(spread(values, ("grp", "x", "core")), axis=0)
    return spread(repeated(part, "z"), "z")


def least_squares(columns, beta):
    ortho = []
    upper = []
    for k in range(len(columns)):
        vector = columns[k]
        coeffs = []
        for i in range(k):
            weight = sum(a * b for a, b in zip(ortho[i], columns[k]))
            coeffs.append(weight)
            vector = [a - weight * b for a, b in zip(vector, ortho[i])]
        length = jnp.sqrt(sum(a * a for a in vector))
        coeffs.append(length)
        upper.append(coeffs)
        ortho.append([a / length for a in vector])
    result = [None] * len(columns)
    for k in reversed(range(len(columns))):
        value = ortho[k][0] * beta
        for i in range(k + 1, len(columns)):
            value = value - upper[i][k] * result[i]
        result[k] = value / upper[k][k]
    return result


def combine(gram):
    size = ITERS + 1
    full = [[gram[min(i, j)][max(i, j)] for j in range(size)] for i in range(size)]
    zero = jnp.zeros_like(full[0][0])

    def inner(a, b):
        return sum(
            a[i] * sum(full[i][j] * b[j] for j in range(size) if b[j] is not None)
            for i in range(size)
            if a[i] is not None
        )

    beta = jnp.sqrt(full[0][0])
    vectors = [[1.0 / beta] + [None] * ITERS]
    columns = []
    for step in range(ITERS):
        image = [None] + [None if c is None else c * (1.0 / SHRINK) for c in vectors[step][:ITERS]]
        square = inner(image, image)
        dots = [inner(vec, image) for vec in vectors]
        heights = sum(d * d for d in dots)
        height = jnp.sqrt(jnp.maximum(square - heights, 0.001 * square))
        columns.append(dots + [height] + [zero] * (ITERS - step - 1))
        rest = []
        for m in range(size):
            terms = [(dots[i], vectors[i][m]) for i in range(step + 1) if vectors[i][m] is not None]
            if image[m] is None and not terms:
                rest.append(None)
                continue
            value = zero if image[m] is None else image[m]
            for dot, factor in terms:
                value = value - dot * factor
            rest.append(value / height)
        vectors.append(rest)
    weights = least_squares(columns, beta)
    return [
        sum(weights[i] * vectors[i][m] for i in range(ITERS) if vectors[i][m] is not None)
        for m in range(ITERS)
    ]


def shape(*dims, dtype=F32):
    return jax.ShapeDtypeStruct(dims, dtype)


def per_device(rhs, diagonal, blocks, pattern, margin, basis, coarse_inverse):
    source = rhs[0, 0]
    diag_row = diagonal[0]
    pattern = pattern[0, 0]
    margin = margin[0, 0]
    basis = basis[0, 0]
    inverse = coarse_inverse[0]
    count, rows = source.shape
    gen = basis.shape[0]
    nblocks, knz = pattern.shape
    groups, zs, xs = lax.axis_size("grp"), lax.axis_size("z"), lax.axis_size("x")
    subs = lax.axis_size(SUB)
    rim = margin.shape[1] * LANES
    core = lax.axis_index("core").astype(jnp.int32).reshape(1)
    vertical = [(2 * g, 2 * g + 2) for g in range(groups - 1)]
    vertical += [(2 * g + 3, 2 * g + 1) for g in range(groups - 1)]
    across = [(i, ((i + 1) ^ 1) - 1) for i in range(1, subs - 1)]
    wide = subs * HALF

    chips = zs * xs
    anywhere = pl.BlockSpec(memory_space=pl.ANY)

    piece = call(
        start_kernel,
        shape(chips, count // 2, LANES),
        [smem(), anywhere, anywhere],
        3_000_000,
        1_500_000,
        [
            pltpu.VMEM((count, rows), F32),
            pltpu.VMEM((gen, rows), F32),
            pltpu.SemaphoreType.DMA((2,)),
        ],
        60,
    )(core, source, basis)
    basis_t, basis_h, inv_row, weights = call(
        prepare_kernel,
        [
            shape(rows, LANES, dtype=BF16),
            shape(gen, 2 * rows, dtype=BF16),
            shape(1, rows),
            shape(nblocks, 4 * HALF, LANES, dtype=BF16),
        ],
        [vmem()] * 3,
        2_000_000,
        6_000_000,
    )(basis, diag_row, blocks[0, 0])
    coarse = call(
        coarse_kernel, shape(wide, LANES, dtype=BF16), [anywhere, vmem()], 1_000_000, 3_200_000
    )(inv_row, inverse)

    krylov = [source]
    conditioned = []
    sums = None
    for step in range(ITERS):
        pieces = spread(piece, ("z", "x"))
        if step == 0:
            pieces, weights = lax.optimization_barrier((pieces, weights))
        pieces = lax.all_gather(pieces, "core")
        p, rims, send_across = call(
            field_kernel,
            [shape(count, rows), shape(3, count, rim), shape(count, rim)],
            [smem(), smem()] + [vmem()] * 5,
            8_000_000,
            3_500_000,
            [pltpu.VMEM((2 * count, wide), BF16)],
        )(core, margin, pieces, krylov[-1], inv_row, coarse, basis_h)
        conditioned.append(p)
        other = lax.ppermute(send_across, SUB, across)
        pair = lax.all_gather(rims, "core")
        carried = lax.dynamic_index_in_dim(pair, core[0], axis=1, keepdims=False)
        carried = lax.ppermute(carried, ("grp", "core"), vertical)
        base = call(
            local_kernel,
            shape(count, rows),
            [smem()] + [vmem()] * 3,
            20_000_000,
            2_500_000,
            [pltpu.VMEM((nblocks, 2 * count, LANES), BF16)] * 2,
        )(pattern, p, diag_row, weights)
        shared = (core, margin, base, lax.all_gather(carried, "core"), other, pair)
        if step < ITERS - 1:
            field, piece = call(
                functools.partial(next_kernel, gen),
                [shape(count, rows), shape(chips, count // 2, LANES)],
                [smem(), smem()] + [vmem()] * 5,
                4_000_000,
                1_000_000,
            )(*shared, basis_t)
            krylov.append(field)
        else:
            sums = call(
                gram_kernel,
                shape(groups * xs * 2, 1, LANES),
                [smem(), smem()] + [vmem()] * 7,
                400_000,
                500_000,
                [pltpu.VMEM((count, rows), F32)],
            )(*shared, *krylov)
    result = call(finish_kernel, shape(count, rows), [vmem()] * 4, 100_000, 300_000)(
        total(sums), *conditioned
    )
    return result[None, None]


def solution(mesh):
    groups = mesh.shape["grp"]
    split = Mesh(mesh.devices.reshape(groups, -1, 4, 2), ("grp",) + SUB)
    specs = (
        P("grp", SUB, None, None),
        P("grp", SUB, None),
        P("grp", SUB, None, None, None, None),
        P("grp", SUB, None, None),
        P("grp", SUB, None, None),
        P("grp", SUB, None, None),
        P("grp", SUB, None),
    )
    return jax.shard_map(
        per_device, mesh=split, in_specs=specs, out_specs=P("grp", SUB, None, None), check_vma=False
    )
```
